32 devices in a mesh: seq: 8 (over y, x, core), dp: 4 (over z).
Axes of the slice: x: 2, y: 2, z: 4, core: 2. Of those that a mesh axis runs over, the one named last changes fastest.
Arguments:
- queries: bfloat16 [4, 1024, 4096], P('dp', 'seq'), may hold values from -6 to 6
- keys: bfloat16 [4, 1024, 512], P('dp', 'seq'), may hold values from -6 to 6
- values: bfloat16 [4, 1024, 512], P('dp', 'seq'), may hold values from -6 to 6
- attn_out: bfloat16 [4, 1024, 4096], P('dp', 'seq'), may hold values from -6 to 6
- out_grad: bfloat16 [4, 1024, 4096], P('dp', 'seq'), may hold values from -6 to 6
- segments: int32 [4, 1024], P('dp', 'seq'), may hold values from 0 to 7, never falling along the last dimension, each value on 1 to 256 neighbouring positions
- token_counts: int32 [4], P('dp'), may hold values from 341 to 1024
- head_slot: int32 [32], replicated, may hold values from 0 to 3, as said below
Outputs:
- query_grad: bfloat16 [4, 1024, 4096], P('dp', 'seq')
- key_grad: bfloat16 [4, 1024, 512], P('dp', 'seq')
- value_grad: bfloat16 [4, 1024, 512], P('dp', 'seq')
The draws below stay inside these ranges and needn't reach their ends.
Inputs may be any that keep to these rules, and one draw needn't show every extreme that they name: `segments`: document ids of a packed sequence, never falling along it; a document holds at most 256 tokens. `head_slot`: never falling over the query heads; every KV head is read by at least one query head, groups may differ in size.
All inputs are finite; a program needn't handle non-finite values.
Results may differ from the reference program's by a relative error of at most 0.006.
Values may be sent and summed in bfloat16 or wider, within the bound.
A program may use at most 64 MiB of HBM per device.

```python
import math
import jax
import jax.numpy as jnp
import numpy as np
from jax import lax

HEADS = 32
HEAD_DIM = 128
KV_SLOTS = 4
SEQ = 1024
BATCHES = 4
DOCS = 8
MOST_DOC = 256


def draw_queries(key, part):
    key = jax.random.fold_in(key, 5)
    shape = (BATCHES, SEQ, HEADS, HEAD_DIM)
    base = jnp.clip(jax.random.normal(key, shape, jnp.float32), -4.0, 4.0)
    return base.reshape(BATCHES, SEQ, HEADS * HEAD_DIM).astype(jnp.bfloat16)


def draw_keys(key, part):
    key = jax.random.fold_in(key, 7)
    shape = (BATCHES, SEQ, KV_SLOTS, HEAD_DIM)
    base = jnp.clip(jax.random.normal(key, shape, jnp.float32), -4.0, 4.0)
    return base.reshape(BATCHES, SEQ, KV_SLOTS * HEAD_DIM).astype(jnp.bfloat16)


def draw_token_counts(key, part):
    key = jax.random.fold_in(key, 23)
    order = jax.random.permutation(key, BATCHES).astype(jnp.int32)
    lowest = SEQ // 3
    spacing = (SEQ - lowest) // max(BATCHES - 1, 1)
    jitter = jax.random.randint(jax.random.fold_in(key, 1), (BATCHES,), 0, max(spacing, 1)).astype(jnp.int32)
    inner = jnp.logical_and(order > 0, order < BATCHES - 1)
    counts = lowest + order * (SEQ - lowest) // max(BATCHES - 1, 1) + jnp.where(inner, jitter, 0)
    return jnp.minimum(counts, SEQ).astype(jnp.int32)


def draw_head_slot(key, part):
    key = jax.random.fold_in(key, 31)
    order = jax.random.permutation(key, HEADS - 1).astype(jnp.int32)
    cuts = order[:KV_SLOTS - 1] + 1
    heads = jnp.arange(HEADS, dtype=jnp.int32)
    passed = (cuts[None, :] <= heads[:, None]).astype(jnp.int32)
    return jnp.sum(passed, axis=1).astype(jnp.int32)


def shard_levels(key, shape, pieces, least, top_value):
    def one(dim, shards_of):
        draws = jax.random.uniform(jax.random.fold_in(jax.random.fold_in(key, 6), dim), (shards_of,), jnp.float32, least / len(pieces), top_value / len(pieces))
        return jnp.repeat(jnp.exp(draws), shape[dim] // shards_of).reshape((-1,) + (1,) * (len(shape) - dim - 1))

    factor_of = one(*pieces[0])
    for cut in pieces[1:]:
        factor_of = factor_of * one(*cut)
    return factor_of


def profile(number_of, total, limit, lean):
    weights = [(1 << 20) // math.isqrt(standing ** lean) + 1 for standing in range(2, number_of + 1)]
    surplus, given = total - limit - (number_of - 1), [1] * (number_of - 1)
    while surplus > 0:
        free = [i for i in range(number_of - 1) if given[i] < limit]
        pool, left = sum([weights[i] for i in free]), surplus
        for i in free:
            extra = min(limit - given[i], max(1, left * weights[i] // pool), surplus)
            given[i] = given[i] + extra
            surplus = surplus - extra
    return np.array([limit] + given)


def uneven_parts(rng, amount, total, bound, lean):
    if amount == 2:
        one = jax.random.randint(rng, (), max(1, total - bound), min(bound, total - 1) + 1)
        return jnp.stack([one, total - one])
    tallies = jnp.asarray(profile(amount, total, bound, lean), jnp.int32)
    twos = (amount - 1) // 2
    source_of, sink = tallies[1:1 + 2 * twos:2], tallies[2:2 + 2 * twos:2]
    slack = jnp.minimum(source_of - 1, bound - sink)
    shifted = jax.random.randint(jax.random.fold_in(rng, 1), (twos,), 0, 1 << 20) % (slack + 1)
    tallies = tallies.at[1:1 + 2 * twos:2].set(source_of - shifted).at[2:2 + 2 * twos:2].set(sink + shifted)
    return tallies[jax.random.permutation(jax.random.fold_in(rng, 2), amount)]


def scatter_about(key, extent, spread, reach, pieces=(), held_as=jnp.bfloat16):
    entries = jax.random.normal(key, extent, jnp.float32) * spread
    if len(pieces) > 0:
        entries = shard_levels(key, extent, pieces, -0.22, 0.18) * entries
    return jnp.clip(entries, min=-reach, max=reach).astype(held_as)


def setup_inputs(seed: int = 0) -> dict:
    seeds = jax.random.split(jax.random.key(seed), 9)
    return {
        "queries": draw_queries(jax.random.fold_in(seeds[8], 71), 0),
        "keys": draw_keys(jax.random.fold_in(seeds[8], 71), 0),
        "values": scatter_about(seeds[2], (BATCHES, SEQ, KV_SLOTS * HEAD_DIM), 1.0, 6.0, ((0, 4), (1, 8))),
        "attn_out": scatter_about(seeds[3], (BATCHES, SEQ, HEADS * HEAD_DIM), 1.0, 6.0, ((0, 4), (1, 8))),
        "out_grad": scatter_about(seeds[4], (BATCHES, SEQ, HEADS * HEAD_DIM), 1.0, 6.0, ((0, 4), (1, 8))),
        "segments": jax.vmap(lambda own: jnp.searchsorted(jnp.cumsum(uneven_parts(own, DOCS, SEQ, MOST_DOC, 0)), jnp.arange(SEQ), side="right"))(jax.random.split(seeds[5], BATCHES)).reshape((BATCHES, SEQ)).astype(jnp.int32),
        "token_counts": draw_token_counts(jax.random.fold_in(seeds[8], 71), 0),
        "head_slot": draw_head_slot(jax.random.fold_in(seeds[8], 71), 0),
    }


NEG_FILL = -1e+30

def contract_rows(left, right):
    return lax.dot_general(left, right, (((1,), (1,)), ((), ())), preferred_element_type=jnp.float32)

def contract_cols(left, right):
    return lax.dot_general(left, right, (((0,), (0,)), ((), ())), preferred_element_type=jnp.float32)

def head_grads(query, key_rows, value_rows, grad_rows, row_delta, doc_ids):
    length, width = query.shape
    tile_rows = min(512, length)
    tile_count = length // tile_rows
    score_scale = 1.0 / math.sqrt(width)

    def rows_of(array, tile):
        return lax.dynamic_slice_in_dim(array, tile * tile_rows, tile_rows, 0)

    def tile_scores(query_tile, q_tile, k_tile):
        key_tile = rows_of(key_rows, k_tile)
        scores = contract_rows(query_tile, key_tile) * score_scale
        q_pos = q_tile * tile_rows + lax.broadcasted_iota(jnp.int32, (tile_rows, tile_rows), 0)
        k_pos = k_tile * tile_rows + lax.broadcasted_iota(jnp.int32, (tile_rows, tile_rows), 1)
        q_doc = rows_of(doc_ids, q_tile)
        k_doc = rows_of(doc_ids, k_tile)
        allowed = jnp.logical_and(k_pos <= q_pos, q_doc[:, None] == k_doc[None, :])
        return (key_tile, scores, allowed)

    def tile_live(q_tile, k_tile):
        first_query = lax.dynamic_index_in_dim(doc_ids, q_tile * tile_rows, 0, keepdims=False)
        last_key = lax.dynamic_index_in_dim(doc_ids, k_tile * tile_rows + tile_rows - 1, 0, keepdims=False)
        return jnp.logical_and(k_tile <= q_tile, last_key >= first_query)
    tiles = jnp.arange(tile_count, dtype=jnp.int32)

    def row_stats(q_tile):
        query_tile = rows_of(query, q_tile)

        def visit_tile(k_tile, running):

            def live_tile(tile_state):
                run_max, run_sum = tile_state
                _, scores, allowed = tile_scores(query_tile, q_tile, k_tile)
                scores = jnp.where(allowed, scores, NEG_FILL)
                new_max = jnp.maximum(run_max, lax.optimization_barrier(jnp.max(scores, axis=1)))
                probs = jnp.where(allowed, jnp.exp(scores - new_max[:, None]), 0.0)
                return (new_max, run_sum * jnp.exp(run_max - new_max) + lax.optimization_barrier(jnp.sum(probs, axis=1)))
            return lax.cond(tile_live(q_tile, k_tile), live_tile, lambda tile_state: tile_state, running)
        start_state = (jnp.full((tile_rows,), NEG_FILL, jnp.float32), jnp.zeros((tile_rows,), jnp.float32))
        run_max, run_sum = lax.fori_loop(jnp.int32(0), jnp.int32(tile_count), visit_tile, start_state)
        return run_max + jnp.log(run_sum)
    log_sums = lax.map(row_stats, tiles)

    def query_pass(running, q_tile):
        key_total, value_total = running
        query_tile = rows_of(query, q_tile)
        grad_tile = rows_of(grad_rows, q_tile)
        delta_tile = rows_of(row_delta, q_tile)
        log_tile = lax.dynamic_index_in_dim(log_sums, q_tile, 0, keepdims=False)

        def visit_tile(k_tile, tile_state):

            def live_tile(inner):
                query_acc, key_acc, value_acc = inner
                key_tile, scores, allowed = tile_scores(query_tile, q_tile, k_tile)
                value_tile = rows_of(value_rows, k_tile)
                weights = jnp.where(allowed, jnp.exp(scores - log_tile[:, None]), 0.0)
                weights_half = weights.astype(jnp.bfloat16)
                value_add = contract_cols(weights_half, grad_tile)
                grad_weights = contract_rows(grad_tile, value_tile)
                score_grad = (weights * (grad_weights - delta_tile[:, None]) * score_scale).astype(jnp.bfloat16)
                query_acc = query_acc + jnp.dot(score_grad, key_tile, preferred_element_type=jnp.float32)
                key_add = contract_cols(score_grad, query_tile)
                start = k_tile * tile_rows
                key_acc = lax.dynamic_update_slice_in_dim(key_acc, rows_of(key_acc, k_tile) + key_add, start, 0)
                value_acc = lax.dynamic_update_slice_in_dim(value_acc, rows_of(value_acc, k_tile) + value_add, start, 0)
                return (query_acc, key_acc, value_acc)
            return lax.cond(tile_live(q_tile, k_tile), live_tile, lambda inner: inner, tile_state)
        start_state = (jnp.zeros((tile_rows, width), jnp.float32), key_total, value_total)
        query_acc, key_total, value_total = lax.fori_loop(jnp.int32(0), jnp.int32(tile_count), visit_tile, start_state)
        return ((key_total, value_total), query_acc)
    zero_rows = jnp.zeros((length, width), jnp.float32)
    (key_total, value_total), query_parts = lax.scan(query_pass, (zero_rows, zero_rows), tiles)
    return (query_parts.reshape(length, width), key_total, value_total)

def reference(queries, keys, values, attn_out, out_grad, segments, token_counts, head_slot):
    token_total = jnp.sum(token_counts.astype(jnp.float32))
    factor = BATCHES * SEQ / token_total
    slot_of = head_slot.astype(jnp.int32)
    one_hot = (slot_of[:, None] == jnp.arange(KV_SLOTS, dtype=jnp.int32)[None, :]).astype(jnp.float32)

    def per_batch(batch):
        query_all = queries[batch].reshape(SEQ, HEADS, HEAD_DIM)
        grad_all = out_grad[batch].reshape(SEQ, HEADS, HEAD_DIM)
        out_all = attn_out[batch].reshape(SEQ, HEADS, HEAD_DIM)
        key_all = keys[batch].reshape(SEQ, KV_SLOTS, HEAD_DIM)
        value_all = values[batch].reshape(SEQ, KV_SLOTS, HEAD_DIM)
        doc_ids = segments[batch]
        delta_all = lax.optimization_barrier(jnp.sum(grad_all.astype(jnp.float32) * out_all.astype(jnp.float32), axis=2))

        def per_head(head):
            slot = slot_of[head]
            query_grad, key_part, value_part = head_grads(lax.dynamic_index_in_dim(query_all, head, 1, keepdims=False), lax.dynamic_index_in_dim(key_all, slot, 1, keepdims=False), lax.dynamic_index_in_dim(value_all, slot, 1, keepdims=False), lax.dynamic_index_in_dim(grad_all, head, 1, keepdims=False), lax.dynamic_index_in_dim(delta_all, head, 1, keepdims=False), doc_ids)
            return ((factor * query_grad).astype(jnp.bfloat16), (factor * key_part).astype(jnp.bfloat16), (factor * value_part).astype(jnp.bfloat16))
        query_heads, key_heads, value_heads = lax.map(per_head, jnp.arange(HEADS, dtype=jnp.int32))
        query_grad = jnp.transpose(query_heads, (1, 0, 2)).reshape(SEQ, HEADS * HEAD_DIM)
        key_grad = jnp.einsum('hsd,hg->sgd', key_heads.astype(jnp.float32), one_hot, precision=lax.Precision.HIGHEST)
        value_grad = jnp.einsum('hsd,hg->sgd', value_heads.astype(jnp.float32), one_hot, precision=lax.Precision.HIGHEST)
        return (query_grad, key_grad.astype(jnp.bfloat16).reshape(SEQ, KV_SLOTS * HEAD_DIM), value_grad.astype(jnp.bfloat16).reshape(SEQ, KV_SLOTS * HEAD_DIM))
    query_grad, key_grad, value_grad = lax.map(per_batch, jnp.arange(BATCHES, dtype=jnp.int32))
    return (query_grad, key_grad, value_grad)
```

```python
import functools
import math

import jax
import jax.numpy as jnp
from jax import lax
from jax.experimental import pallas as pl
from jax.experimental.pallas import tpu as pltpu
from jax.sharding import PartitionSpec as P

HEADS = 32
HEAD_DIM = 128
KV_SLOTS = 4
WIDTH = HEADS * HEAD_DIM
KV_WIDTH = KV_SLOTS * HEAD_DIM
NEG_FILL = -1e30
SCALE = 1.0 / math.sqrt(HEAD_DIM)
EXP2_SCALE = SCALE / math.log(2.0)
MESH = pl.DeviceIdType.MESH


def dot(left, right, dims):
    return lax.dot_general(left, right, (dims, ((), ())), preferred_element_type=jnp.float32)


def block_diag(both):
    first, second = both[:, :HEAD_DIM], both[:, HEAD_DIM:]
    zero = jnp.zeros_like(first)
    return jnp.concatenate(
        [jnp.concatenate([first, zero], axis=1), jnp.concatenate([zero, second], axis=1)], axis=0
    )


def kernel(
    n, ndp, rows,
    q_hbm, k_hbm, v_hbm, o_hbm, g_hbm, seg_ref, cnt_ref, slot_ref,
    dq_ref, dk_ref, dv_ref,
    qbuf, gbuf, obuf, kbuf, vbuf, kslot, vslot, ktslot, sbuf, cbuf, bias,
    acc_k, acc_v, back, home,
    local_sem, kv_send, kv_recv, cnt_send, cnt_recv, back_send, back_recv,
):
    halo = n // 4
    me = lax.axis_index("seq")
    my_dp = lax.axis_index("dp")

    loads = [
        pltpu.make_async_copy(k_hbm, kbuf.at[pl.ds(halo * rows, rows)], local_sem.at[0]),
        pltpu.make_async_copy(v_hbm, vbuf.at[pl.ds(halo * rows, rows)], local_sem.at[1]),
        pltpu.make_async_copy(q_hbm, qbuf, local_sem.at[2]),
        pltpu.make_async_copy(g_hbm, gbuf, local_sem.at[3]),
        pltpu.make_async_copy(o_hbm, obuf, local_sem.at[4]),
    ]
    for load in loads:
        load.start()

    barrier = pltpu.get_barrier_semaphore()
    for j in range(1, halo + 1):
        for other in (me + j, me - j):
            @pl.when(jnp.logical_and(other >= 0, other < n))
            def _():
                pl.semaphore_signal(barrier, inc=1, device_id={"seq": other}, device_id_type=MESH)
    for j in range(1, ndp):
        pl.semaphore_signal(
            barrier, inc=1, device_id={"dp": lax.rem(my_dp + j, ndp)}, device_id_type=MESH
        )
    pl.semaphore_wait(
        barrier, jnp.minimum(me, halo) + jnp.minimum(n - 1 - me, halo) + (ndp - 1)
    )

    def halo_copies(j):
        target = {"seq": me + j}
        place = pl.ds((halo - j) * rows, rows)
        return [
            pltpu.make_async_remote_copy(
                src, dst, kv_send.at[j - 1, i], kv_recv.at[j - 1, i],
                device_id=target, device_id_type=MESH,
            )
            for i, (src, dst) in enumerate(
                [
                    (k_hbm, kbuf.at[place]),
                    (v_hbm, vbuf.at[place]),
                    (seg_ref, sbuf.at[halo - j]),
                ]
            )
        ]

    for j in range(halo, 0, -1):
        @pl.when(me + j < n)
        def _():
            for copy in halo_copies(j):
                copy.start()

    cbuf[0] = jnp.full((8, 128), cnt_ref[0].astype(jnp.float32))

    def count_copy(j):
        return pltpu.make_async_remote_copy(
            cbuf.at[0], cbuf.at[j], cnt_send.at[j], cnt_recv.at[j],
            device_id={"dp": lax.rem(my_dp + j, ndp)}, device_id_type=MESH,
        )

    for j in range(1, ndp):
        count_copy(j).start()

    sbuf[halo] = seg_ref[...]
    for j in range(1, halo + 1):
        @pl.when(me - j < 0)
        def _():
            kbuf[pl.ds((halo - j) * rows, rows), :] = jnp.zeros((rows, KV_WIDTH), jnp.bfloat16)
            vbuf[pl.ds((halo - j) * rows, rows), :] = jnp.zeros((rows, KV_WIDTH), jnp.bfloat16)
            sbuf[halo - j] = jnp.full((1, rows), -1, jnp.int32)

    for load in loads:
        load.wait()
    for j in range(1, ndp):
        count_copy(j).wait_recv()
    for j in range(1, halo + 1):
        @pl.when(me - j >= 0)
        def _():
            for copy in halo_copies(j):
                copy.wait_recv()

    total = cbuf[0]
    for j in range(1, ndp):
        total = total + cbuf[j]
    factor = (float(ndp * n * rows) / total)[0:1, :]
    scaled = factor * SCALE

    q_doc = seg_ref[...].astype(jnp.float32)
    for b in range(halo + 1):
        k_doc = jnp.transpose(jnp.broadcast_to(sbuf[b].astype(jnp.float32), (rows, rows)))
        allowed = k_doc == q_doc
        if b == halo:
            k_pos = lax.broadcasted_iota(jnp.int32, (rows, rows), 0)
            q_pos = lax.broadcasted_iota(jnp.int32, (rows, rows), 1)
            allowed = jnp.logical_and(allowed, k_pos <= q_pos)
        one = jnp.where(allowed, 0.0, NEG_FILL)
        place = pl.ds(b * rows, rows)
        bias[place, :] = jnp.concatenate([one, one], axis=1)
        for s in range(KV_SLOTS):
            lanes = pl.ds(s * HEAD_DIM, HEAD_DIM)
            tile = kbuf[place, lanes]
            kslot[s, place, :] = tile
            ktslot[s, :, place] = jnp.transpose(tile)
            vslot[s, place, :] = vbuf[place, lanes]

    def pair(p, carry):
        h1 = 2 * p
        h2 = h1 + 1
        s1, s2 = slot_ref[h1], slot_ref[h2]
        before = slot_ref[lax.rem(h1 + HEADS - 1, HEADS)]
        keep1 = jnp.where(before == s1, 1.0, 0.0)
        keep2 = jnp.where(s1 == s2, 1.0, 0.0)
        cols = pl.ds(pl.multiple_of(p * 2 * HEAD_DIM, 2 * HEAD_DIM), 2 * HEAD_DIM)
        q2, g2, o2 = qbuf[:, cols], gbuf[:, cols], obuf[:, cols]
        q_diag, g_diag = block_diag(q2), block_diag(g2)
        k_cat = jnp.concatenate([kslot[s1], kslot[s2]], axis=1)
        v_cat = jnp.concatenate([vslot[s1], vslot[s2]], axis=1)

        product = g2.astype(jnp.float32) * o2.astype(jnp.float32)
        high = product.astype(jnp.bfloat16)
        low = (product - high.astype(jnp.float32)).astype(jnp.bfloat16)
        terms = jnp.concatenate(
            [
                jnp.concatenate([high[:, :HEAD_DIM], low[:, :HEAD_DIM]], axis=1),
                jnp.concatenate([high[:, HEAD_DIM:], low[:, HEAD_DIM:]], axis=1),
            ],
            axis=0,
        )
        ones = jnp.ones((16, 2 * HEAD_DIM), jnp.bfloat16)
        delta = dot(ones, terms, ((1,), (1,)))[0:1, :]

        scores = dot(k_cat, q_diag, ((1,), (1,))) + bias[...]
        top = jnp.max(scores, axis=0, keepdims=True)
        expd = jnp.exp2((scores - top) * EXP2_SCALE)
        weights = expd * (1.0 / jnp.sum(expd, axis=0, keepdims=True))
        grad_weights = dot(v_cat, g_diag, ((1,), (1,)))
        score_grad = (weights * (grad_weights - delta)).astype(jnp.bfloat16)

        v_part = dot(weights.astype(jnp.bfloat16), g_diag, ((1,), (0,)))
        k_part = dot(score_grad, q_diag, ((1,), (0,)))
        for acc, part in ((acc_k, k_part), (acc_v, v_part)):
            first = acc[h1] * keep1 + part[:, :HEAD_DIM]
            acc[h1 + 1] = first
            acc[h1 + 2] = first * keep2 + part[:, HEAD_DIM:]

        turned = []
        for i, s in enumerate((s1, s2)):
            dqt = dot(ktslot[s], score_grad[:, i * HEAD_DIM:(i + 1) * HEAD_DIM], ((1,), (0,)))
            turned.append((jnp.transpose(dqt) * scaled).astype(jnp.bfloat16))
        dq_ref[:, cols] = jnp.concatenate(turned, axis=1)
        return carry

    acc_k[0] = jnp.zeros(acc_k.shape[1:], jnp.float32)
    acc_v[0] = jnp.zeros(acc_v.shape[1:], jnp.float32)
    lax.fori_loop(0, HEADS // 2, pair, 0)

    lasts = [jnp.int32(0)] * KV_SLOTS
    for h in range(HEADS):
        slot = slot_ref[h]
        lasts = [last + (slot <= s).astype(jnp.int32) for s, last in enumerate(lasts)]

    def back_copy(j):
        return pltpu.make_async_remote_copy(
            back.at[j - 1], home.at[j - 1], back_send.at[j - 1], back_recv.at[j - 1],
            device_id={"seq": me - j}, device_id_type=MESH,
        )

    for j in range(halo, 0, -1):
        place = pl.ds((halo - j) * rows, rows)
        for s in range(KV_SLOTS):
            lanes = pl.ds(s * HEAD_DIM, HEAD_DIM)
            back[j - 1, 0, :, lanes] = (acc_k[lasts[s], place, :] * scaled).astype(jnp.bfloat16)
            back[j - 1, 1, :, lanes] = (acc_v[lasts[s], place, :] * factor).astype(jnp.bfloat16)

        @pl.when(me - j >= 0)
        def _():
            back_copy(j).start()

    for j in range(1, halo + 1):
        @pl.when(me + j >= n)
        def _():
            home[j - 1] = jnp.zeros(home.shape[1:], jnp.bfloat16)

        @pl.when(me + j < n)
        def _():
            back_copy(j).wait_recv()

    place = pl.ds(halo * rows, rows)
    for s in range(KV_SLOTS):
        lanes = pl.ds(s * HEAD_DIM, HEAD_DIM)
        for i, (acc, gain, out) in enumerate(((acc_k, scaled, dk_ref), (acc_v, factor, dv_ref))):
            value = acc[lasts[s], place, :] * gain
            for j in range(halo):
                value = value + home[j, i, :, lanes].astype(jnp.float32)
            out[:, lanes] = value.astype(jnp.bfloat16)

    for j in range(1, ndp):
        count_copy(j).wait_send()
    for j in range(1, halo + 1):
        @pl.when(me + j < n)
        def _():
            for copy in halo_copies(j):
                copy.wait_send()

        @pl.when(me - j >= 0)
        def _():
            back_copy(j).wait_send()


def local(queries, keys, values, attn_out, out_grad, segments, token_counts, head_slot):
    n, ndp = lax.axis_size("seq"), lax.axis_size("dp")
    rows = queries.shape[1]
    halo = n // 4
    span = (halo + 1) * rows
    hbm = pl.BlockSpec(memory_space=pl.ANY)
    vmem = pl.BlockSpec(memory_space=pltpu.VMEM)
    smem = pl.BlockSpec(memory_space=pltpu.SMEM)
    bf16, f32 = jnp.bfloat16, jnp.float32
    dma = pltpu.SemaphoreType.DMA
    dq, dk, dv = pl.pallas_call(
        functools.partial(kernel, n, ndp, rows),
        out_shape=[
            jax.ShapeDtypeStruct((rows, WIDTH), bf16),
            jax.ShapeDtypeStruct((rows, KV_WIDTH), bf16),
            jax.ShapeDtypeStruct((rows, KV_WIDTH), bf16),
        ],
        in_specs=[hbm] * 5 + [vmem, smem, smem],
        out_specs=[vmem] * 3,
        scratch_shapes=[
            pltpu.VMEM((rows, WIDTH), bf16),
            pltpu.VMEM((rows, WIDTH), bf16),
            pltpu.VMEM((rows, WIDTH), bf16),
            pltpu.VMEM((span, KV_WIDTH), bf16),
            pltpu.VMEM((span, KV_WIDTH), bf16),
            pltpu.VMEM((KV_SLOTS, span, HEAD_DIM), bf16),
            pltpu.VMEM((KV_SLOTS, span, HEAD_DIM), bf16),
            pltpu.VMEM((KV_SLOTS, HEAD_DIM, span), bf16),
            pltpu.VMEM((halo + 1, 1, rows), jnp.int32),
            pltpu.VMEM((ndp, 8, 128), f32),
            pltpu.VMEM((span, 2 * HEAD_DIM), f32),
            pltpu.VMEM((HEADS + 1, span, HEAD_DIM), f32),
            pltpu.VMEM((HEADS + 1, span, HEAD_DIM), f32),
            pltpu.VMEM((halo, 2, rows, KV_WIDTH), bf16),
            pltpu.VMEM((halo, 2, rows, KV_WIDTH), bf16),
            dma((5,)),
            dma((halo, 3)),
            dma((halo, 3)),
            dma((ndp,)),
            dma((ndp,)),
            dma((halo,)),
            dma((halo,)),
        ],
        compiler_params=pltpu.CompilerParams(
            collective_id=0, has_side_effects=True, vmem_limit_bytes=60 * 1024 * 1024
        ),
    )(queries[0], keys[0], values[0], attn_out[0], out_grad[0], segments, token_counts, head_slot)
    return dq[None], dk[None], dv[None]


def solution(mesh):
    in_specs = (
        P("dp", "seq", None),
        P("dp", "seq", None),
        P("dp", "seq", None),
        P("dp", "seq", None),
        P("dp", "seq", None),
        P("dp", "seq"),
        P("dp"),
        P(),
    )
    out_specs = (P("dp", "seq", None), P("dp", "seq", None), P("dp", "seq", None))
    return jax.shard_map(local, mesh=mesh, in_specs=in_specs, out_specs=out_specs, check_vma=False)
```

```python
import functools
import math

import jax
import jax.numpy as jnp
from jax import lax
from jax.experimental import pallas as pl
from jax.experimental.pallas import tpu as pltpu
from jax.sharding import PartitionSpec as P

HEADS = 32
HEAD_DIM = 128
KV_SLOTS = 4
WIDTH = HEADS * HEAD_DIM
KV_WIDTH = KV_SLOTS * HEAD_DIM
NEG_FILL = -1e30
SCALE = 1.0 / math.sqrt(HEAD_DIM)
EXP2_SCALE = SCALE / math.log(2.0)
MESH = pl.DeviceIdType.MESH
UNROLL = 4


def dot(left, right, dims):
    return lax.dot_general(left, right, (dims, ((), ())), preferred_element_type=jnp.float32)


def block_diag(both):
    first, second = both[:, :HEAD_DIM], both[:, HEAD_DIM:]
    zero = jnp.zeros_like(first)
    return jnp.concatenate(
        [jnp.concatenate([first, zero], axis=1), jnp.concatenate([zero, second], axis=1)], axis=0
    )


def kernel(
    n, ndp, rows,
    q_hbm, k_hbm, v_hbm, o_hbm, g_hbm, seg_ref, cnt_ref, slot_ref,
    dq_hbm, dk_ref, dv_ref,
    qbuf, gbuf, obuf, kbuf, vbuf, kslot, vslot, ktslot, sbuf, cbuf, bias,
    acc_k, acc_v, mix, home, own_exp, own_grad, early_score_grad, early_query, top, norm, delta,
    local_sem, kv_send, kv_recv, pass_send, cnt_send, cnt_recv, swap_send, swap_recv,
    back_send, back_recv,
):
    halo = n // 4
    me = lax.axis_index("seq")
    my_dp = lax.axis_index("dp")

    loads = [
        pltpu.make_async_copy(k_hbm, kbuf.at[pl.ds(halo * rows, rows)], local_sem.at[0]),
        pltpu.make_async_copy(v_hbm, vbuf.at[pl.ds(halo * rows, rows)], local_sem.at[1]),
        pltpu.make_async_copy(q_hbm, qbuf, local_sem.at[2]),
        pltpu.make_async_copy(g_hbm, gbuf, local_sem.at[3]),
        pltpu.make_async_copy(o_hbm, obuf, local_sem.at[4]),
    ]
    for load in loads:
        load.start()

    barrier = pltpu.get_barrier_semaphore()
    for j in range(1, halo + 1):
        for other in (me + j, me - j):
            @pl.when(jnp.logical_and(other >= 0, other < n))
            def _():
                pl.semaphore_signal(barrier, inc=1, device_id={"seq": other}, device_id_type=MESH)
    for j in range(1, ndp):
        pl.semaphore_signal(
            barrier, inc=1, device_id={"dp": lax.rem(my_dp + j, ndp)}, device_id_type=MESH
        )
    pl.semaphore_wait(
        barrier, jnp.minimum(me, halo) + jnp.minimum(n - 1 - me, halo) + (ndp - 1)
    )

    odd = lax.rem(me, 2) == 1

    def when(*terms):
        terms = [term for term in terms if term is not True]
        if any(term is False for term in terms):
            return lambda body: None
        return pl.when(functools.reduce(jnp.logical_and, terms))

    def block(j):
        return pl.ds((halo - j) * rows, rows)

    def crosses(j, later_odd):
        later_even = jnp.logical_not(later_odd)
        return (True if j == 1 else later_even, True if j == halo else later_odd)

    def passes_on(j):
        return (
            jnp.logical_not(odd) if j < halo else False,
            odd if j > 1 else False,
        )

    def kv_copy(i, j):
        return pltpu.make_async_remote_copy(
            (k_hbm, v_hbm)[i], (kbuf, vbuf)[i].at[block(j)],
            kv_send.at[j - 1, i], kv_recv.at[j - 1, i],
            device_id={"seq": me + j}, device_id_type=MESH,
        )

    def seg_copy(j):
        return pltpu.make_async_remote_copy(
            seg_ref, sbuf.at[halo - j], kv_send.at[j - 1, 2], kv_recv.at[j - 1, 2],
            device_id={"seq": me + j}, device_id_type=MESH,
        )

    def pass_copy(i, j):
        step = 1 - 2 * i
        buf = (kbuf, vbuf)[i]
        return pltpu.make_async_remote_copy(
            buf.at[block(j)], buf.at[block(j + step)],
            pass_send.at[j - 1, i], kv_recv.at[j + step - 1, i],
            device_id={"seq": me + step}, device_id_type=MESH,
        )

    for j in range(halo, 0, -1):
        later_odd = lax.rem(me + j, 2) == 1
        for i in range(2):
            @when(me + j < n, crosses(j, later_odd)[i])
            def _():
                kv_copy(i, j).start()

        @when(me + j < n)
        def _():
            seg_copy(j).start()

    cbuf[0] = jnp.full((8, 128), cnt_ref[0].astype(jnp.float32))

    def count_copy(j):
        return pltpu.make_async_remote_copy(
            cbuf.at[0], cbuf.at[j], cnt_send.at[j], cnt_recv.at[j],
            device_id={"dp": lax.rem(my_dp + j, ndp)}, device_id_type=MESH,
        )

    for j in range(1, ndp):
        count_copy(j).start()

    sbuf[halo] = seg_ref[...]
    for j in range(1, halo + 1):
        @pl.when(me - j < 0)
        def _():
            kbuf[pl.ds((halo - j) * rows, rows), :] = jnp.zeros((rows, KV_WIDTH), jnp.bfloat16)
            vbuf[pl.ds((halo - j) * rows, rows), :] = jnp.zeros((rows, KV_WIDTH), jnp.bfloat16)
            sbuf[halo - j] = jnp.full((1, rows), -1, jnp.int32)

    q_doc = seg_ref[...].astype(jnp.float32)

    def prepare(b):
        k_doc = jnp.transpose(jnp.broadcast_to(sbuf[b].astype(jnp.float32), (rows, rows)))
        allowed = k_doc == q_doc
        if b == halo:
            k_pos = lax.broadcasted_iota(jnp.int32, (rows, rows), 0)
            q_pos = lax.broadcasted_iota(jnp.int32, (rows, rows), 1)
            allowed = jnp.logical_and(allowed, k_pos <= q_pos)
        one = jnp.where(allowed, 0.0, NEG_FILL)
        place = pl.ds(b * rows, rows)
        bias[place, :] = jnp.concatenate([one, one], axis=1)
        for s in range(KV_SLOTS):
            lanes = pl.ds(s * HEAD_DIM, HEAD_DIM)
            tile = kbuf[place, lanes]
            kslot[s, place, :] = tile
            ktslot[s, :, place] = jnp.transpose(tile)
            vslot[s, place, :] = vbuf[place, lanes]

    def pair_cols(p):
        return pl.ds(pl.multiple_of(p * 2 * HEAD_DIM, 2 * HEAD_DIM), 2 * HEAD_DIM)

    def both_slots(buf, p, place):
        first, second = slot_ref[2 * p], slot_ref[2 * p + 1]
        return jnp.concatenate([buf[first, place, :], buf[second, place, :]], axis=1)

    def accumulate(p, place, k_part, v_part):
        h1 = 2 * p
        s1, s2 = slot_ref[h1], slot_ref[h1 + 1]
        before = slot_ref[lax.rem(h1 + HEADS - 1, HEADS)]
        keep1 = jnp.where(before == s1, 1.0, 0.0)
        keep2 = jnp.where(s1 == s2, 1.0, 0.0)
        for acc, part in ((acc_k, k_part), (acc_v, v_part)):
            first = acc[h1, place, :] * keep1 + part[:, :HEAD_DIM]
            acc[h1 + 1, place, :] = first
            acc[h1 + 2, place, :] = first * keep2 + part[:, HEAD_DIM:]

    own = pl.ds(halo * rows, rows)
    early = pl.ds(0, halo * rows)

    def own_scores(p):
        cols = pair_cols(p)
        q2, g2, o2 = qbuf[:, cols], gbuf[:, cols], obuf[:, cols]
        q_diag, g_diag = block_diag(q2), block_diag(g2)
        product = g2.astype(jnp.float32) * o2.astype(jnp.float32)
        high = product.astype(jnp.bfloat16)
        low = (product - high.astype(jnp.float32)).astype(jnp.bfloat16)
        terms = jnp.concatenate(
            [
                jnp.concatenate([high[:, :HEAD_DIM], low[:, :HEAD_DIM]], axis=1),
                jnp.concatenate([high[:, HEAD_DIM:], low[:, HEAD_DIM:]], axis=1),
            ],
            axis=0,
        )
        ones = jnp.ones((16, 2 * HEAD_DIM), jnp.bfloat16)
        row_delta = dot(ones, terms, ((1,), (1,)))[0:1, :]
        scores = dot(both_slots(kslot, p, own), q_diag, ((1,), (1,))) + bias[own, :]
        peak = jnp.max(scores, axis=0, keepdims=True)
        expd = jnp.exp2((scores - peak) * EXP2_SCALE)
        own_exp[p] = expd
        own_grad[p] = dot(both_slots(vslot, p, own), g_diag, ((1,), (1,))) - row_delta
        top[p] = peak
        norm[p] = jnp.sum(expd, axis=0, keepdims=True)
        delta[p] = row_delta

    def early_grads(p):
        cols = pair_cols(p)
        q_diag, g_diag = block_diag(qbuf[:, cols]), block_diag(gbuf[:, cols])
        scores = dot(both_slots(kslot, p, early), q_diag, ((1,), (1,))) + bias[early, :]
        own_top = top[p]
        peak = jnp.maximum(own_top, jnp.max(scores, axis=0, keepdims=True))
        expd = jnp.exp2((scores - peak) * EXP2_SCALE)
        shrink = jnp.exp2((own_top - peak) * EXP2_SCALE)
        inverse = 1.0 / (jnp.sum(expd, axis=0, keepdims=True) + norm[p] * shrink)
        norm[p] = shrink * inverse
        weights = expd * inverse
        grad_weights = dot(both_slots(vslot, p, early), g_diag, ((1,), (1,)))
        score_grad = (weights * (grad_weights - delta[p])).astype(jnp.bfloat16)
        if halo <= 2:
            early_score_grad[p] = score_grad
        else:
            for i in range(2):
                kt = ktslot[slot_ref[2 * p + i], :, early]
                early_query[p, i] = dot(kt, score_grad[:, i * HEAD_DIM:(i + 1) * HEAD_DIM], ((1,), (0,)))
        accumulate(
            p, early,
            dot(score_grad, q_diag, ((1,), (0,))),
            dot(weights.astype(jnp.bfloat16), g_diag, ((1,), (0,))),
        )

    def own_grads(p):
        cols = pair_cols(p)
        q_diag, g_diag = block_diag(qbuf[:, cols]), block_diag(gbuf[:, cols])
        weights = own_exp[p] * norm[p]
        score_grad = (weights * own_grad[p]).astype(jnp.bfloat16)
        accumulate(
            p, own,
            dot(score_grad, q_diag, ((1,), (0,))),
            dot(weights.astype(jnp.bfloat16), g_diag, ((1,), (0,))),
        )
        turned = []
        for i in range(2):
            lanes = slice(i * HEAD_DIM, (i + 1) * HEAD_DIM)
            slot = slot_ref[2 * p + i]
            if halo <= 2:
                every = jnp.concatenate([early_score_grad[p], score_grad], axis=0)
                dqt = dot(ktslot[slot], every[:, lanes], ((1,), (0,)))
            else:
                dqt = early_query[p, i] + dot(ktslot[slot, :, own], score_grad[:, lanes], ((1,), (0,)))
            turned.append((jnp.transpose(dqt) * scaled).astype(jnp.bfloat16))
        qbuf[:, cols] = jnp.concatenate(turned, axis=1)

    def all_pairs(step, first=0, last=4):
        unroll = UNROLL if halo <= 2 else 1

        def body(i, carry):
            for u in range(unroll):
                step(i * unroll + u)
            return carry

        quarter = HEADS // 8 // unroll
        lax.fori_loop(first * quarter, last * quarter, body, 0)

    acc_k[0] = jnp.zeros(acc_k.shape[1:], jnp.float32)
    acc_v[0] = jnp.zeros(acc_v.shape[1:], jnp.float32)
    for load in loads:
        load.wait()
    prepare(halo)
    all_pairs(own_scores)

    for j in range(1, ndp):
        count_copy(j).wait_recv()
    total = cbuf[0]
    for j in range(1, ndp):
        total = total + cbuf[j]
    factor = (float(ndp * n * rows) / total)[0:1, :]
    scaled = factor * SCALE

    for j in range(1, halo + 1):
        for i in range(2):
            @when(me - j >= 0, passes_on(j)[i])
            def _():
                kv_copy(i, j).wait_recv()
                pass_copy(i, j).start()

    for j in range(1, halo + 1):
        @when(me - j >= 0)
        def _():
            seg_copy(j).wait_recv()

        for i in range(2):
            @when(me - j >= 0, True if passes_on(j)[i] is False else jnp.logical_not(passes_on(j)[i]))
            def _():
                kv_copy(i, j).wait_recv()

        prepare(halo - j)
    all_pairs(early_grads)

    lasts = [jnp.int32(0)] * KV_SLOTS
    for h in range(HEADS):
        slot = slot_ref[h]
        lasts = [last + (slot <= s).astype(jnp.int32) for s, last in enumerate(lasts)]

    def part(i, j, s):
        return (acc_k, acc_v)[i][lasts[s], block(j), :] * (scaled, factor)[i]

    def back_copy(i, j):
        return pltpu.make_async_remote_copy(
            (kbuf, vbuf)[i].at[block(j)], home.at[j - 1, i],
            back_send.at[j - 1, i], back_recv.at[j - 1, i],
            device_id={"seq": me - j}, device_id_type=MESH,
        )

    def swap_copy(i, j):
        place = j - 2 if i == 0 else j - 1
        return pltpu.make_async_remote_copy(
            (kbuf, vbuf)[i].at[block(j)], mix.at[place], swap_send.at[place], swap_recv.at[place],
            device_id={"seq": me - 1 if i == 0 else me + 1}, device_id_type=MESH,
        )

    def stage(i, j, place=None):
        for s in range(KV_SLOTS):
            lanes = pl.ds(s * HEAD_DIM, HEAD_DIM)
            value = part(i, j, s)
            if place is not None:
                value = value + mix[place, :, lanes].astype(jnp.float32)
            (kbuf, vbuf)[i][block(j), lanes] = value.astype(jnp.bfloat16)

    even = jnp.logical_not(odd)
    for j in range(1, halo + 1):
        for i in range(2):
            @when(me - j >= 0, passes_on(j)[i])
            def _():
                pass_copy(i, j).wait_send()

    for j in range(1, halo + 1):
        @when(me - j >= 0, even, j < halo)
        def _():
            stage(1, j)
            swap_copy(1, j).start()

        @when(me - j >= 0, odd, j > 1)
        def _():
            stage(0, j)
            swap_copy(0, j).start()

    for j, mine in ((halo, even), (1, odd)):
        @when(me - j >= 0, mine)
        def _():
            for i in range(2):
                stage(i, j)
                back_copy(i, j).start()

    all_pairs(own_grads, 0, 1)

    for j in range(1, halo + 1):
        @when(me - j >= 0, even, j < halo)
        def _():
            swap_copy(0, j + 1).wait_recv()
            stage(0, j, j - 1)
            back_copy(0, j).start()

        @when(me - j >= 0, odd, j > 1)
        def _():
            swap_copy(1, j - 1).wait_recv()
            stage(1, j, j - 2)
            back_copy(1, j).start()

    all_pairs(own_grads, 1, 4)
    store_dq = pltpu.make_async_copy(qbuf, dq_hbm, local_sem.at[2])
    store_dq.start()

    for j in range(1, halo + 1):
        later_odd = lax.rem(me + j, 2) == 1
        for i in range(2):
            sent = crosses(j, later_odd)[i]

            @when(me + j < n, sent)
            def _():
                back_copy(i, j).wait_recv()

            @pl.when(jnp.logical_not(jnp.logical_and(me + j < n, sent)))
            def _():
                home[j - 1, i] = jnp.zeros(home.shape[2:], jnp.bfloat16)

    place = pl.ds(halo * rows, rows)
    for s in range(KV_SLOTS):
        lanes = pl.ds(s * HEAD_DIM, HEAD_DIM)
        for i, (acc, gain, out) in enumerate(((acc_k, scaled, dk_ref), (acc_v, factor, dv_ref))):
            value = acc[lasts[s], place, :] * gain
            for j in range(halo):
                value = value + home[j, i, :, lanes].astype(jnp.float32)
            out[:, lanes] = value.astype(jnp.bfloat16)

    store_dq.wait()
    for j in range(1, ndp):
        count_copy(j).wait_send()
    for j in range(1, halo + 1):
        later_odd = lax.rem(me + j, 2) == 1

        @when(me + j < n)
        def _():
            seg_copy(j).wait_send()

        for i in range(2):
            @when(me + j < n, crosses(j, later_odd)[i])
            def _():
                kv_copy(i, j).wait_send()

            @when(me - j >= 0, crosses(j, odd)[i])
            def _():
                back_copy(i, j).wait_send()

        @when(me - j >= 0, even, j < halo)
        def _():
            swap_copy(1, j).wait_send()

        @when(me - j >= 0, odd, j > 1)
        def _():
            swap_copy(0, j).wait_send()


def local(queries, keys, values, attn_out, out_grad, segments, token_counts, head_slot):
    n, ndp = lax.axis_size("seq"), lax.axis_size("dp")
    rows = queries.shape[1]
    halo = n // 4
    span = (halo + 1) * rows
    hbm = pl.BlockSpec(memory_space=pl.ANY)
    vmem = pl.BlockSpec(memory_space=pltpu.VMEM)
    smem = pl.BlockSpec(memory_space=pltpu.SMEM)
    bf16, f32 = jnp.bfloat16, jnp.float32
    dma = pltpu.SemaphoreType.DMA
    dq, dk, dv = pl.pallas_call(
        functools.partial(kernel, n, ndp, rows),
        out_shape=[
            jax.ShapeDtypeStruct((rows, WIDTH), bf16),
            jax.ShapeDtypeStruct((rows, KV_WIDTH), bf16),
            jax.ShapeDtypeStruct((rows, KV_WIDTH), bf16),
        ],
        in_specs=[hbm] * 5 + [vmem, smem, smem],
        out_specs=[hbm, vmem, vmem],
        scratch_shapes=[
            pltpu.VMEM((rows, WIDTH), bf16),
            pltpu.VMEM((rows, WIDTH), bf16),
            pltpu.VMEM((rows, WIDTH), bf16),
            pltpu.VMEM((span, KV_WIDTH), bf16),
            pltpu.VMEM((span, KV_WIDTH), bf16),
            pltpu.VMEM((KV_SLOTS, span, HEAD_DIM), bf16),
            pltpu.VMEM((KV_SLOTS, span, HEAD_DIM), bf16),
            pltpu.VMEM((KV_SLOTS, HEAD_DIM, span), bf16),
            pltpu.VMEM((halo + 1, 1, rows), jnp.int32),
            pltpu.VMEM((ndp, 8, 128), f32),
            pltpu.VMEM((span, 2 * HEAD_DIM), f32),
            pltpu.VMEM((HEADS + 1, span, HEAD_DIM), f32),
            pltpu.VMEM((HEADS + 1, span, HEAD_DIM), f32),
            pltpu.VMEM((halo - 1, rows, KV_WIDTH), bf16),
            pltpu.VMEM((halo, 2, rows, KV_WIDTH), bf16),
            pltpu.VMEM((HEADS // 2, rows, 2 * HEAD_DIM), f32),
            pltpu.VMEM((HEADS // 2, rows, 2 * HEAD_DIM), f32),
            pltpu.VMEM((HEADS // 2 if halo <= 2 else 1, halo * rows, 2 * HEAD_DIM), bf16),
            pltpu.VMEM((1 if halo <= 2 else HEADS // 2, 2, HEAD_DIM, rows), f32),
            pltpu.VMEM((HEADS // 2, 1, 2 * HEAD_DIM), f32),
            pltpu.VMEM((HEADS // 2, 1, 2 * HEAD_DIM), f32),
            pltpu.VMEM((HEADS // 2, 1, 2 * HEAD_DIM), f32),
            dma((5,)),
            dma((halo, 3)),
            dma((halo, 3)),
            dma((halo, 2)),
            dma((ndp,)),
            dma((ndp,)),
            dma((halo - 1,)),
            dma((halo - 1,)),
            dma((halo, 2)),
            dma((halo, 2)),
        ],
        compiler_params=pltpu.CompilerParams(
            collective_id=0, has_side_effects=True, vmem_limit_bytes=60 * 1024 * 1024
        ),
    )(queries[0], keys[0], values[0], attn_out[0], out_grad[0], segments, token_counts, head_slot)
    return dq[None], dk[None], dv[None]


def solution(mesh):
    in_specs = (
        P("dp", "seq", None),
        P("dp", "seq", None),
        P("dp", "seq", None),
        P("dp", "seq", None),
        P("dp", "seq", None),
        P("dp", "seq"),
        P("dp"),
        P(),
    )
    out_specs = (P("dp", "seq", None), P("dp", "seq", None), P("dp", "seq", None))
    return jax.shard_map(local, mesh=mesh, in_specs=in_specs, out_specs=out_specs, check_vma=False)
```

```python
import functools
import math

import jax
import jax.numpy as jnp
from jax import lax
from jax.experimental import pallas as pl
from jax.experimental.pallas import tpu as pltpu
from jax.sharding import PartitionSpec as P

HEADS = 32
HEAD_DIM = 128
KV_SLOTS = 4
WIDTH = HEADS * HEAD_DIM
KV_WIDTH = KV_SLOTS * HEAD_DIM
NEG_FILL = -1e30
SCALE = 1.0 / math.sqrt(HEAD_DIM)
EXP2_SCALE = SCALE / math.log(2.0)
MESH = pl.DeviceIdType.MESH
UNROLL = 4


def dot(left, right, dims):
    return lax.dot_general(left, right, (dims, ((), ())), preferred_element_type=jnp.float32)


def block_diag(both):
    first, second = both[:, :HEAD_DIM], both[:, HEAD_DIM:]
    zero = jnp.zeros_like(first)
    return jnp.concatenate(
        [jnp.concatenate([first, zero], axis=1), jnp.concatenate([zero, second], axis=1)], axis=0
    )


def kernel(
    n, ndp, rows,
    q_hbm, k_hbm, v_hbm, o_hbm, g_hbm, seg_ref, cnt_ref, slot_ref,
    dq_hbm, dk_ref, dv_ref,
    qbuf, gbuf, obuf, kbuf, vbuf, kslot, vslot, ktslot, sbuf, cbuf, bias,
    acc_k, acc_v, mix, home, own_exp, own_grad, early_score_grad, early_query, top, norm, delta,
    local_sem, kv_send, kv_recv, pass_send, cnt_send, cnt_recv, swap_send, swap_recv,
    back_send, back_recv,
):
    halo = n // 4
    me = lax.axis_index("seq")
    my_dp = lax.axis_index("dp")

    loads = [
        pltpu.make_async_copy(k_hbm, kbuf.at[pl.ds(halo * rows, rows)], local_sem.at[0]),
        pltpu.make_async_copy(v_hbm, vbuf.at[pl.ds(halo * rows, rows)], local_sem.at[1]),
        pltpu.make_async_copy(q_hbm, qbuf, local_sem.at[2]),
        pltpu.make_async_copy(g_hbm, gbuf, local_sem.at[3]),
        pltpu.make_async_copy(o_hbm, obuf, local_sem.at[4]),
    ]
    for load in loads:
        load.start()

    barrier = pltpu.get_barrier_semaphore()
    for j in range(1, halo + 1):
        for other in (me + j, me - j):
            @pl.when(jnp.logical_and(other >= 0, other < n))
            def _():
                pl.semaphore_signal(barrier, inc=1, device_id={"seq": other}, device_id_type=MESH)
    for j in range(1, ndp):
        pl.semaphore_signal(
            barrier, inc=1, device_id={"dp": lax.rem(my_dp + j, ndp)}, device_id_type=MESH
        )
    pl.semaphore_wait(
        barrier, jnp.minimum(me, halo) + jnp.minimum(n - 1 - me, halo) + (ndp - 1)
    )

    odd = lax.rem(me, 2) == 1

    def when(*terms):
        terms = [term for term in terms if term is not True]
        if any(term is False for term in terms):
            return lambda body: None
        return pl.when(functools.reduce(jnp.logical_and, terms))

    def block(j):
        return pl.ds((halo - j) * rows, rows)

    def crosses(j, later_odd):
        later_even = jnp.logical_not(later_odd)
        return (True if j == 1 else later_even, True if j == halo else later_odd)

    def passes_on(j):
        return (
            jnp.logical_not(odd) if j < halo else False,
            odd if j > 1 else False,
        )

    def kv_copy(i, j):
        return pltpu.make_async_remote_copy(
            (k_hbm, v_hbm)[i], (kbuf, vbuf)[i].at[block(j)],
            kv_send.at[j - 1, i], kv_recv.at[j - 1, i],
            device_id={"seq": me + j}, device_id_type=MESH,
        )

    def seg_copy(j):
        return pltpu.make_async_remote_copy(
            seg_ref, sbuf.at[halo - j], kv_send.at[j - 1, 2], kv_recv.at[j - 1, 2],
            device_id={"seq": me + j}, device_id_type=MESH,
        )

    def pass_copy(i, j):
        step = 1 - 2 * i
        buf = (kbuf, vbuf)[i]
        return pltpu.make_async_remote_copy(
            buf.at[block(j)], buf.at[block(j + step)],
            pass_send.at[j - 1, i], kv_recv.at[j + step - 1, i],
            device_id={"seq": me + step}, device_id_type=MESH,
        )

    for j in range(halo, 0, -1):
        later_odd = lax.rem(me + j, 2) == 1
        for i in range(2):
            @when(me + j < n, crosses(j, later_odd)[i])
            def _():
                kv_copy(i, j).start()

        @when(me + j < n)
        def _():
            seg_copy(j).start()

    cbuf[0] = jnp.full((8, 128), cnt_ref[0].astype(jnp.float32))

    def count_copy(j):
        return pltpu.make_async_remote_copy(
            cbuf.at[0], cbuf.at[j], cnt_send.at[j], cnt_recv.at[j],
            device_id={"dp": lax.rem(my_dp + j, ndp)}, device_id_type=MESH,
        )

    for j in range(1, ndp):
        count_copy(j).start()

    sbuf[halo] = seg_ref[...]
    for j in range(1, halo + 1):
        @pl.when(me - j < 0)
        def _():
            kbuf[pl.ds((halo - j) * rows, rows), :] = jnp.zeros((rows, KV_WIDTH), jnp.bfloat16)
            vbuf[pl.ds((halo - j) * rows, rows), :] = jnp.zeros((rows, KV_WIDTH), jnp.bfloat16)
            sbuf[halo - j] = jnp.full((1, rows), -1, jnp.int32)

    q_doc = seg_ref[...].astype(jnp.float32)

    def prepare(b):
        k_doc = jnp.transpose(jnp.broadcast_to(sbuf[b].astype(jnp.float32), (rows, rows)))
        allowed = k_doc == q_doc
        if b == halo:
            k_pos = lax.broadcasted_iota(jnp.int32, (rows, rows), 0)
            q_pos = lax.broadcasted_iota(jnp.int32, (rows, rows), 1)
            allowed = jnp.logical_and(allowed, k_pos <= q_pos)
        one = jnp.where(allowed, 0.0, NEG_FILL)
        place = pl.ds(b * rows, rows)
        bias[place, :] = jnp.concatenate([one, one], axis=1)
        for s in range(KV_SLOTS):
            lanes = pl.ds(s * HEAD_DIM, HEAD_DIM)
            kslot[s, place, :] = kbuf[place, lanes]
            vslot[s, place, :] = vbuf[place, lanes]

    def turn_keys(b):
        place = pl.ds(b * rows, rows)
        for s in range(KV_SLOTS):
            ktslot[s, :, place] = jnp.transpose(kslot[s, place, :])

    def pair_cols(p):
        return pl.ds(pl.multiple_of(p * 2 * HEAD_DIM, 2 * HEAD_DIM), 2 * HEAD_DIM)

    def both_slots(buf, p, place):
        first, second = slot_ref[2 * p], slot_ref[2 * p + 1]
        return jnp.concatenate([buf[first, place, :], buf[second, place, :]], axis=1)

    def accumulate(p, place, k_part, v_part):
        h1 = 2 * p
        s1, s2 = slot_ref[h1], slot_ref[h1 + 1]
        before = slot_ref[lax.rem(h1 + HEADS - 1, HEADS)]
        keep1 = jnp.where(before == s1, 1.0, 0.0)
        keep2 = jnp.where(s1 == s2, 1.0, 0.0)
        for acc, part in ((acc_k, k_part), (acc_v, v_part)):
            first = acc[h1, place, :] * keep1 + part[:, :HEAD_DIM]
            acc[h1 + 1, place, :] = first
            acc[h1 + 2, place, :] = first * keep2 + part[:, HEAD_DIM:]

    own = pl.ds(halo * rows, rows)
    early = pl.ds(0, halo * rows)

    def own_scores(p):
        cols = pair_cols(p)
        q2, g2, o2 = qbuf[:, cols], gbuf[:, cols], obuf[:, cols]
        q_diag, g_diag = block_diag(q2), block_diag(g2)
        product = g2.astype(jnp.float32) * o2.astype(jnp.float32)
        high = product.astype(jnp.bfloat16)
        low = (product - high.astype(jnp.float32)).astype(jnp.bfloat16)
        terms = jnp.concatenate(
            [
                jnp.concatenate([high[:, :HEAD_DIM], low[:, :HEAD_DIM]], axis=1),
                jnp.concatenate([high[:, HEAD_DIM:], low[:, HEAD_DIM:]], axis=1),
            ],
            axis=0,
        )
        ones = jnp.ones((16, 2 * HEAD_DIM), jnp.bfloat16)
        row_delta = dot(ones, terms, ((1,), (1,)))[0:1, :]
        scores = dot(both_slots(kslot, p, own), q_diag, ((1,), (1,))) + bias[own, :]
        peak = jnp.max(scores, axis=0, keepdims=True)
        expd = jnp.exp2((scores - peak) * EXP2_SCALE)
        own_exp[p] = expd
        own_grad[p] = dot(both_slots(vslot, p, own), g_diag, ((1,), (1,))) - row_delta
        top[p] = peak
        norm[p] = jnp.sum(expd, axis=0, keepdims=True)
        delta[p] = row_delta

    def early_grads(p):
        cols = pair_cols(p)
        q_diag, g_diag = block_diag(qbuf[:, cols]), block_diag(gbuf[:, cols])
        scores = dot(both_slots(kslot, p, early), q_diag, ((1,), (1,))) + bias[early, :]
        own_top = top[p]
        peak = jnp.maximum(own_top, jnp.max(scores, axis=0, keepdims=True))
        expd = jnp.exp2((scores - peak) * EXP2_SCALE)
        shrink = jnp.exp2((own_top - peak) * EXP2_SCALE)
        inverse = 1.0 / (jnp.sum(expd, axis=0, keepdims=True) + norm[p] * shrink)
        norm[p] = shrink * inverse
        weights = expd * inverse
        grad_weights = dot(both_slots(vslot, p, early), g_diag, ((1,), (1,)))
        score_grad = (weights * (grad_weights - delta[p])).astype(jnp.bfloat16)
        if halo <= 2:
            early_score_grad[p] = score_grad
        else:
            for i in range(2):
                kt = ktslot[slot_ref[2 * p + i], :, early]
                early_query[p, i] = dot(kt, score_grad[:, i * HEAD_DIM:(i + 1) * HEAD_DIM], ((1,), (0,)))
        accumulate(
            p, early,
            dot(score_grad, q_diag, ((1,), (0,))),
            dot(weights.astype(jnp.bfloat16), g_diag, ((1,), (0,))),
        )

    def own_grads(p):
        cols = pair_cols(p)
        q_diag, g_diag = block_diag(qbuf[:, cols]), block_diag(gbuf[:, cols])
        weights = own_exp[p] * norm[p]
        score_grad = (weights * own_grad[p]).astype(jnp.bfloat16)
        accumulate(
            p, own,
            dot(score_grad, q_diag, ((1,), (0,))),
            dot(weights.astype(jnp.bfloat16), g_diag, ((1,), (0,))),
        )
        turned = []
        for i in range(2):
            lanes = slice(i * HEAD_DIM, (i + 1) * HEAD_DIM)
            slot = slot_ref[2 * p + i]
            if halo <= 2:
                every = jnp.concatenate([early_score_grad[p], score_grad], axis=0)
                dqt = dot(ktslot[slot], every[:, lanes], ((1,), (0,)))
            else:
                dqt = early_query[p, i] + dot(ktslot[slot, :, own], score_grad[:, lanes], ((1,), (0,)))
            turned.append((jnp.transpose(dqt) * scaled).astype(jnp.bfloat16))
        qbuf[:, cols] = jnp.concatenate(turned, axis=1)

    def all_pairs(step, first=0, last=4):
        unroll = UNROLL if halo <= 2 else 1

        def body(i, carry):
            for u in range(unroll):
                step(i * unroll + u)
            return carry

        quarter = HEADS // 8 // unroll
        lax.fori_loop(first * quarter, last * quarter, body, 0)

    acc_k[0] = jnp.zeros(acc_k.shape[1:], jnp.float32)
    acc_v[0] = jnp.zeros(acc_v.shape[1:], jnp.float32)
    for load in loads:
        load.wait()
    lasts = [jnp.int32(0)] * KV_SLOTS
    for h in range(HEADS):
        slot = slot_ref[h]
        lasts = [last + (slot <= s).astype(jnp.int32) for s, last in enumerate(lasts)]

    prepare(halo)
    turn_keys(halo)
    all_pairs(own_scores)

    for j in range(1, ndp):
        count_copy(j).wait_recv()
    total = cbuf[0]
    for j in range(1, ndp):
        total = total + cbuf[j]
    factor = (float(ndp * n * rows) / total)[0:1, :]
    scaled = factor * SCALE

    for j in range(1, halo + 1):
        for i in range(2):
            @when(me - j >= 0, passes_on(j)[i])
            def _():
                kv_copy(i, j).wait_recv()
                pass_copy(i, j).start()

    for j in range(1, halo + 1):
        @when(me - j >= 0)
        def _():
            seg_copy(j).wait_recv()

        for i in range(2):
            @when(me - j >= 0, True if passes_on(j)[i] is False else jnp.logical_not(passes_on(j)[i]))
            def _():
                kv_copy(i, j).wait_recv()

        prepare(halo - j)
        if halo > 2:
            turn_keys(halo - j)
    all_pairs(early_grads)

    def part(i, j, s):
        return (acc_k, acc_v)[i][lasts[s], block(j), :] * (scaled, factor)[i]

    def back_copy(i, j):
        return pltpu.make_async_remote_copy(
            (kbuf, vbuf)[i].at[block(j)], home.at[j - 1, i],
            back_send.at[j - 1, i], back_recv.at[j - 1, i],
            device_id={"seq": me - j}, device_id_type=MESH,
        )

    def swap_copy(i, j):
        place = j - 2 if i == 0 else j - 1
        return pltpu.make_async_remote_copy(
            (kbuf, vbuf)[i].at[block(j)], mix.at[place], swap_send.at[place], swap_recv.at[place],
            device_id={"seq": me - 1 if i == 0 else me + 1}, device_id_type=MESH,
        )

    def stage(i, j, place=None):
        for s in range(KV_SLOTS):
            lanes = pl.ds(s * HEAD_DIM, HEAD_DIM)
            value = part(i, j, s)
            if place is not None:
                value = value + mix[place, :, lanes].astype(jnp.float32)
            (kbuf, vbuf)[i][block(j), lanes] = value.astype(jnp.bfloat16)

    even = jnp.logical_not(odd)
    for j in range(1, halo + 1):
        for i in range(2):
            @when(me - j >= 0, passes_on(j)[i])
            def _():
                pass_copy(i, j).wait_send()

    for j in range(1, halo + 1):
        @when(me - j >= 0, even, j < halo)
        def _():
            stage(1, j)
            swap_copy(1, j).start()

        @when(me - j >= 0, odd, j > 1)
        def _():
            stage(0, j)
            swap_copy(0, j).start()

    for j, mine in ((halo, even), (1, odd)):
        @when(me - j >= 0, mine)
        def _():
            for i in range(2):
                stage(i, j)
                back_copy(i, j).start()

    if halo <= 2:
        for j in range(1, halo + 1):
            turn_keys(halo - j)
    all_pairs(own_grads, 0, 1)

    for j in range(1, halo + 1):
        @when(me - j >= 0, even, j < halo)
        def _():
            swap_copy(0, j + 1).wait_recv()
            stage(0, j, j - 1)
            back_copy(0, j).start()

        @when(me - j >= 0, odd, j > 1)
        def _():
            swap_copy(1, j - 1).wait_recv()
            stage(1, j, j - 2)
            back_copy(1, j).start()

    all_pairs(own_grads, 1, 4)
    store_dq = pltpu.make_async_copy(qbuf, dq_hbm, local_sem.at[2])
    store_dq.start()

    for j in range(1, halo + 1):
        later_odd = lax.rem(me + j, 2) == 1
        for i in range(2):
            sent = crosses(j, later_odd)[i]

            @when(me + j < n, sent)
            def _():
                back_copy(i, j).wait_recv()

            @pl.when(jnp.logical_not(jnp.logical_and(me + j < n, sent)))
            def _():
                home[j - 1, i] = jnp.zeros(home.shape[2:], jnp.bfloat16)

    place = pl.ds(halo * rows, rows)
    for s in range(KV_SLOTS):
        lanes = pl.ds(s * HEAD_DIM, HEAD_DIM)
        for i, (acc, gain, out) in enumerate(((acc_k, scaled, dk_ref), (acc_v, factor, dv_ref))):
            value = acc[lasts[s], place, :] * gain
            for j in range(halo):
                value = value + home[j, i, :, lanes].astype(jnp.float32)
            out[:, lanes] = value.astype(jnp.bfloat16)

    store_dq.wait()
    for j in range(1, ndp):
        count_copy(j).wait_send()
    for j in range(1, halo + 1):
        later_odd = lax.rem(me + j, 2) == 1

        @when(me + j < n)
        def _():
            seg_copy(j).wait_send()

        for i in range(2):
            @when(me + j < n, crosses(j, later_odd)[i])
            def _():
                kv_copy(i, j).wait_send()

            @when(me - j >= 0, crosses(j, odd)[i])
            def _():
                back_copy(i, j).wait_send()

        @when(me - j >= 0, even, j < halo)
        def _():
            swap_copy(1, j).wait_send()

        @when(me - j >= 0, odd, j > 1)
        def _():
            swap_copy(0, j).wait_send()


PIECES = 4


def settle(dq_in, dk_in, dv_in, dq_out, dk_out, dv_out, dq_held, dk_held, dv_held, sems):
    rows = dq_in.shape[0] // PIECES
    moves = []
    for i in range(PIECES):
        place = pl.ds(i * rows, rows)
        moves.append((dq_in.at[place], dq_held.at[place], dq_out.at[place]))
    moves.append((dk_in, dk_held, dk_out))
    moves.append((dv_in, dv_held, dv_out))
    reads = [pltpu.make_async_copy(m[0], m[1], sems.at[0, i]) for i, m in enumerate(moves)]
    writes = [pltpu.make_async_copy(m[1], m[2], sems.at[1, i]) for i, m in enumerate(moves)]
    for read in reads:
        read.start()
    for read, write in zip(reads, writes):
        read.wait()
        write.start()
    for write in writes:
        write.wait()


def local(queries, keys, values, attn_out, out_grad, segments, token_counts, head_slot):
    n, ndp = lax.axis_size("seq"), lax.axis_size("dp")
    rows = queries.shape[1]
    halo = n // 4
    span = (halo + 1) * rows
    hbm = pl.BlockSpec(memory_space=pl.ANY)
    vmem = pl.BlockSpec(memory_space=pltpu.VMEM)
    smem = pl.BlockSpec(memory_space=pltpu.SMEM)
    bf16, f32 = jnp.bfloat16, jnp.float32
    dma = pltpu.SemaphoreType.DMA
    dq, dk, dv = pl.pallas_call(
        functools.partial(kernel, n, ndp, rows),
        out_shape=[
            jax.ShapeDtypeStruct((rows, WIDTH), bf16),
            jax.ShapeDtypeStruct((rows, KV_WIDTH), bf16),
            jax.ShapeDtypeStruct((rows, KV_WIDTH), bf16),
        ],
        in_specs=[hbm] * 5 + [vmem, smem, smem],
        out_specs=[hbm, vmem, vmem],
        scratch_shapes=[
            pltpu.VMEM((rows, WIDTH), bf16),
            pltpu.VMEM((rows, WIDTH), bf16),
            pltpu.VMEM((rows, WIDTH), bf16),
            pltpu.VMEM((span, KV_WIDTH), bf16),
            pltpu.VMEM((span, KV_WIDTH), bf16),
            pltpu.VMEM((KV_SLOTS, span, HEAD_DIM), bf16),
            pltpu.VMEM((KV_SLOTS, span, HEAD_DIM), bf16),
            pltpu.VMEM((KV_SLOTS, HEAD_DIM, span), bf16),
            pltpu.VMEM((halo + 1, 1, rows), jnp.int32),
            pltpu.VMEM((ndp, 8, 128), f32),
            pltpu.VMEM((span, 2 * HEAD_DIM), f32),
            pltpu.VMEM((HEADS + 1, span, HEAD_DIM), f32),
            pltpu.VMEM((HEADS + 1, span, HEAD_DIM), f32),
            pltpu.VMEM((halo - 1, rows, KV_WIDTH), bf16),
            pltpu.VMEM((halo, 2, rows, KV_WIDTH), bf16),
            pltpu.VMEM((HEADS // 2, rows, 2 * HEAD_DIM), f32),
            pltpu.VMEM((HEADS // 2, rows, 2 * HEAD_DIM), f32),
            pltpu.VMEM((HEADS // 2 if halo <= 2 else 1, halo * rows, 2 * HEAD_DIM), bf16),
            pltpu.VMEM((1 if halo <= 2 else HEADS // 2, 2, HEAD_DIM, rows), f32),
            pltpu.VMEM((HEADS // 2, 1, 2 * HEAD_DIM), f32),
            pltpu.VMEM((HEADS // 2, 1, 2 * HEAD_DIM), f32),
            pltpu.VMEM((HEADS // 2, 1, 2 * HEAD_DIM), f32),
            dma((5,)),
            dma((halo, 3)),
            dma((halo, 3)),
            dma((halo, 2)),
            dma((ndp,)),
            dma((ndp,)),
            dma((halo - 1,)),
            dma((halo - 1,)),
            dma((halo, 2)),
            dma((halo, 2)),
        ],
        compiler_params=pltpu.CompilerParams(
            collective_id=0, has_side_effects=True, vmem_limit_bytes=60 * 1024 * 1024
        ),
    )(queries[0], keys[0], values[0], attn_out[0], out_grad[0], segments, token_counts, head_slot)
    dq, dk, dv = pl.pallas_call(
        settle,
        out_shape=[jax.ShapeDtypeStruct(x.shape, bf16) for x in (dq, dk, dv)],
        in_specs=[hbm] * 3,
        out_specs=[hbm] * 3,
        scratch_shapes=[pltpu.VMEM(x.shape, bf16) for x in (dq, dk, dv)] + [dma((2, PIECES + 2))],
    )(dq, dk, dv)
    return dq[None], dk[None], dv[None]


def solution(mesh):
    in_specs = (
        P("dp", "seq", None),
        P("dp", "seq", None),
        P("dp", "seq", None),
        P("dp", "seq", None),
        P("dp", "seq", None),
        P("dp", "seq"),
        P("dp"),
        P(),
    )
    out_specs = (P("dp", "seq", None), P("dp", "seq", None), P("dp", "seq", None))
    return jax.shard_map(local, mesh=mesh, in_specs=in_specs, out_specs=out_specs, check_vma=False)
```
